32 devices in a mesh: seq: 8 (over y, x, core), head: 4 (over z).
Axes of the slice: x: 2, y: 2, z: 4, core: 2. Of those that a mesh axis runs over, the one named last changes fastest.
Arguments:
- inputs_x: bfloat16 [2048, 8192], P('seq', 'head'), may hold values from -6 to 6
- inputs_b: bfloat16 [2048, 1024], P('seq', 'head'), may hold values from -0.59765625 to 0.59765625
- inputs_c: bfloat16 [2048, 1024], P('seq', 'head'), may hold values from -6 to 6
- gate_z: bfloat16 [2048, 8192], P('seq', 'head'), may hold values from -6 to 6
- log_decay: float32 [128, 2048], P('head', 'seq'), may hold values from -1 to 0, as said below
- resets: int32 [2048], P('seq'), may hold values from 0 to 1, as said below
- norm_gain: float32 [8192], P('head'), may hold values from 0.1 to 1.9
- out_weight: bfloat16 [4096, 8192], P('seq', 'head'), may hold values from -0.09375 to 0.09375
- out_grad: bfloat16 [2048, 4096], P('seq', 'head'), may hold values from -6 to 6
Outputs:
- layer_out: bfloat16 [2048, 4096], P('seq', 'head')
- grad_x: float32 [2048, 8192], P('seq', 'head')
- grad_b: float32 [2048, 1024], P('seq', 'head')
- grad_c: float32 [2048, 1024], P('seq', 'head')
- grad_z: float32 [2048, 8192], P('seq', 'head')
- grad_decay: float32 [128, 2048], P('head', 'seq')
- grad_weight: float32 [4096, 8192], P('seq', 'head')
The draws below stay inside these ranges and needn't reach their ends.
Inputs may be any that keep to these rules, and one draw needn't show every extreme that they name: `log_decay`: the decay factor of a token is exp of its entry. `resets`: exactly one entry is 1, the first token of the second rollout, at a position from 256 to 1791.
All inputs are finite; a program needn't handle non-finite values.
Results may differ from the reference program's by a relative error of at most 0.023.
Values may be sent and summed in bfloat16 or wider, within the bound.
A program may use at most 128 MiB of HBM per device.

```python
import jax
import jax.numpy as jnp
from jax import lax

D = 4096
SSD_HALF_LANES = 128
P_SIZE = 64
N = 128
G = 8
SPAN = 256
TOK_DEV = 256
DIALOGUE_SYMBOLS = 2048
HP = 8192
N_SEQ = 8
N_HEAD = 4


def draw_resets(key, part):
    position = jax.random.randint(key, (), DIALOGUE_SYMBOLS // 8, DIALOGUE_SYMBOLS - DIALOGUE_SYMBOLS // 8)
    return (jnp.arange(DIALOGUE_SYMBOLS, dtype=jnp.int32) == position).astype(jnp.int32)


def draw_log_decay(key, part):
    sampler_seeds = jax.random.split(key, 7)
    slow_share = 0.5
    slow = jax.random.uniform(sampler_seeds[0], (SSD_HALF_LANES, 1)) < slow_share
    slow_rate = jax.random.uniform(sampler_seeds[1], (SSD_HALF_LANES, 1), minval=0.3, maxval=1.0) / DIALOGUE_SYMBOLS
    fast_rate = jax.random.uniform(sampler_seeds[2], (SSD_HALF_LANES, 1), minval=0.02, maxval=0.035)
    starting_displacement = jnp.where(slow, slow_rate, fast_rate)
    approximate_guess = jnp.exp(jax.random.uniform(sampler_seeds[3], (SSD_HALF_LANES, DIALOGUE_SYMBOLS), minval=-0.69, maxval=0.69))
    block_count = DIALOGUE_SYMBOLS // TOK_DEV
    segment_multiplier = jnp.exp(jax.random.uniform(sampler_seeds[4], (SSD_HALF_LANES, block_count, 1), minval=-0.69, maxval=0.69))
    segment_multiplier = jnp.broadcast_to(segment_multiplier, (SSD_HALF_LANES, block_count, TOK_DEV)).reshape(SSD_HALF_LANES, DIALOGUE_SYMBOLS)
    segment_number = jax.random.uniform(sampler_seeds[5], (SSD_HALF_LANES, DIALOGUE_SYMBOLS)) < 2.0 / DIALOGUE_SYMBOLS
    segment_extent = jax.random.uniform(sampler_seeds[6], (SSD_HALF_LANES, DIALOGUE_SYMBOLS), minval=0.22, maxval=0.69)
    return (-(starting_displacement * approximate_guess * segment_multiplier + jnp.where(segment_number, segment_extent, 0.0))).astype(jnp.float32)


def with_spikes(array, rng, source, target, shards_of, factor):
    def block_of(axis_at):
        return (jnp.arange(array.shape[axis_at]) // (array.shape[axis_at] // shards_of)).reshape((-1,) + (1,) * (array.ndim - 1 - axis_at))

    one_side = jax.random.permutation(rng, shards_of)[block_of(target)]
    far = (block_of(target) + shards_of // 2) % shards_of
    return jnp.where((block_of(source) == one_side) | (block_of(source) == far), factor * array, array)


def shard_levels(rng, shape, cuts, smallest, top_value):
    def one(dim, parts):
        draws = jax.random.uniform(jax.random.fold_in(jax.random.fold_in(rng, 6), dim), (parts,), jnp.float32, smallest / len(cuts), top_value / len(cuts))
        return jnp.repeat(jnp.exp(draws), shape[dim] // parts).reshape((-1,) + (1,) * (len(shape) - dim - 1))

    level = one(*cuts[0])
    for cut in cuts[1:]:
        level = level * one(*cut)
    return level


def gaussian(rng, dims, scale, bound, shards=(), kind=jnp.bfloat16):
    entries = scale * jax.random.normal(rng, dims, jnp.float32)
    if shards:
        entries = entries * shard_levels(rng, dims, shards, -0.22, 0.18)
    return jnp.clip(entries, -bound, bound).astype(kind)


def heavy_noise(rng, extent, scale, limit, cuts, heavy, kind=jnp.bfloat16):
    values = scale * jax.random.normal(rng, extent, jnp.float32)
    if cuts:
        values = values * shard_levels(rng, extent, cuts, -0.22, 0.18)
    return jnp.clip(with_spikes(values, jax.random.fold_in(rng, 3), *heavy), -limit, limit).astype(kind)


def setup_inputs(seed: int = 0) -> dict:
    key_of = jax.random.split(jax.random.key(seed), 10)
    inputs_x = gaussian(key_of[0], (DIALOGUE_SYMBOLS, HP), 1.0, 6.0, ((0, 8), (1, 4)))
    inputs_b = gaussian(key_of[1], (DIALOGUE_SYMBOLS, G * N), 0.1, 0.59765625, ((0, 8), (1, 4)))
    inputs_c = gaussian(key_of[2], (DIALOGUE_SYMBOLS, G * N), 1.0, 6.0, ((0, 8), (1, 4)))
    gate_z = gaussian(key_of[3], (DIALOGUE_SYMBOLS, HP), 1.0, 6.0, ((0, 8), (1, 4)))
    log_decay = draw_log_decay(jax.random.fold_in(key_of[9], 71), 0)
    resets = draw_resets(jax.random.fold_in(key_of[9], 71), 0)
    norm_gain = jnp.clip(1.0 + 0.18 * jax.random.normal(key_of[6], (HP,), jnp.float32), 0.1, 1.9)
    out_weight = heavy_noise(key_of[7], (D, HP), HP ** -0.5, 0.09375, ((0, 8), (1, 4)), (1, 0, 8, 2.0))
    out_grad = heavy_noise(key_of[8], (DIALOGUE_SYMBOLS, D), 1.0, 6.0, ((0, 8), (1, 4)), (0, 1, 8, 2.0))
    return dict(inputs_x=inputs_x, inputs_b=inputs_b, inputs_c=inputs_c, gate_z=gate_z, log_decay=log_decay, resets=resets, norm_gain=norm_gain, out_weight=out_weight, out_grad=out_grad)


def span_scan(inputs_x, inputs_b, inputs_c, log_decay, resets, start_state):
    tokens_here = inputs_x.shape[0]
    heads_here = log_decay.shape[0]
    groups_here = inputs_b.shape[1] // N
    repeat_count = heads_here // groups_here
    blocks = tokens_here // SPAN
    x_blocks = inputs_x.reshape(blocks, SPAN, heads_here, P_SIZE)
    b_blocks = inputs_b.reshape(blocks, SPAN, groups_here, N)
    c_blocks = inputs_c.reshape(blocks, SPAN, groups_here, N)
    d_blocks = log_decay.reshape(heads_here, blocks, SPAN).transpose(1, 0, 2)
    r_blocks = resets.reshape(blocks, SPAN)
    order = jnp.arange(SPAN, dtype=jnp.int32)
    lower = order[None, :] <= order[:, None]

    def advance(state, pieces):
        x_here, b_here, c_here, d_here, r_here = pieces
        cumul = jnp.cumsum(d_here, axis=1)
        counts = jnp.cumsum(r_here)
        same = lower & (counts[:, None] == counts[None, :])
        spread = cumul[:, :, None] - cumul[:, None, :]
        weights = jnp.where(same[None], jnp.exp(jnp.minimum(spread, 0.0)), 0.0)
        scores = jnp.einsum('tgn,sgn->gts', c_here, b_here, precision=lax.Precision.HIGHEST)
        scores = jnp.repeat(scores, repeat_count, axis=0) * weights
        inner = jnp.einsum('hts,shp->thp', scores, x_here, precision=lax.Precision.HIGHEST)
        c_heads = jnp.repeat(c_here, repeat_count, axis=1)
        b_heads = jnp.repeat(b_here, repeat_count, axis=1)
        entry = jnp.exp(cumul) * (counts == 0).astype(jnp.float32)[None, :]
        carried = jnp.einsum('thn,hpn->thp', c_heads, state, precision=lax.Precision.HIGHEST) * entry.T[:, :, None]
        tail = jnp.exp(cumul[:, -1:] - cumul) * (counts == counts[-1]).astype(jnp.float32)[None, :]
        fresh = jnp.einsum('shp,shn->hpn', x_here * tail.T[:, :, None], b_heads, precision=lax.Precision.HIGHEST)
        passing = entry[:, -1]
        return (fresh + passing[:, None, None] * state, inner + carried)
    final, outputs = lax.scan(jax.checkpoint(advance), start_state, (x_blocks, b_blocks, c_blocks, d_blocks, r_blocks))
    return (outputs.reshape(tokens_here, heads_here * P_SIZE), final)

def gated_norm(values, gate, gain):
    gated = values * jax.nn.silu(gate)
    rows_here, width = gated.shape
    group_width = HP // G
    grouped = gated.reshape(rows_here, width // group_width, group_width)
    scale = lax.rsqrt(lax.optimization_barrier(jnp.mean(grouped * grouped, axis=2, keepdims=True)) + 1e-05)
    return (grouped * scale).reshape(rows_here, width) * gain[None, :]

def reference(inputs_x, inputs_b, inputs_c, gate_z, log_decay, resets, norm_gain, out_weight, out_grad):
    start_state = jnp.zeros((SSD_HALF_LANES, P_SIZE, N), jnp.float32)

    def forward(x_float, b_float, c_float, z_float, decay_arg):
        values, unused_final = span_scan(x_float, b_float, c_float, decay_arg, resets, start_state)
        return gated_norm(values, z_float, norm_gain)
    normed, pullback = jax.vjp(forward, inputs_x.astype(jnp.float32), inputs_b.astype(jnp.float32), inputs_c.astype(jnp.float32), gate_z.astype(jnp.float32), log_decay)
    normed_bf = normed.astype(jnp.bfloat16)
    width_dev = HP // N_HEAD
    total = jnp.zeros((DIALOGUE_SYMBOLS, D), jnp.float32)
    for shard_index in range(N_HEAD):
        low = shard_index * width_dev
        part_term = lax.dot_general(normed_bf[:, low:low + width_dev], out_weight[:, low:low + width_dev], (((1,), (1,)), ((), ())), preferred_element_type=jnp.float32)
        total = total + lax.optimization_barrier(part_term.astype(jnp.bfloat16)).astype(jnp.float32)
    layer_out = total.astype(jnp.bfloat16)
    grad_y = jnp.dot(out_grad, out_weight, preferred_element_type=jnp.float32)
    grad_weight = jnp.zeros((D, HP), jnp.float32)
    for block_index in range(N_SEQ):
        low = block_index * TOK_DEV
        weight_term = lax.dot_general(out_grad[low:low + TOK_DEV], normed_bf[low:low + TOK_DEV], (((0,), (0,)), ((), ())), preferred_element_type=jnp.float32)
        grad_weight = grad_weight + lax.optimization_barrier(weight_term.astype(jnp.bfloat16)).astype(jnp.float32)
    grad_x, grad_b, grad_c, grad_z, grad_decay = pullback(grad_y)
    return (layer_out, grad_x, grad_b, grad_c, grad_z, grad_decay, grad_weight)
```

```python
import jax
import jax.numpy as jnp
from jax import lax
from jax.experimental import pallas as pl
from jax.experimental.pallas import tpu as pltpu
from jax.sharding import PartitionSpec as P

P_SIZE = 64
N = 128
GROUP = 1024
HEADS = GROUP // P_SIZE
ROWS = HEADS + 8
F32 = jnp.float32
BF16 = jnp.bfloat16
NN = (((1,), (0,)), ((), ()))
NT = (((1,), (1,)), ((), ()))
TN = (((0,), (0,)), ((), ()))


def mm(a, b, dims=NN):
    return lax.dot_general(a, b, dims, preferred_element_type=F32)


def exact(a, b, dims=NN):
    return lax.dot_general(
        a, b, dims, preferred_element_type=F32, precision=lax.Precision.HIGHEST
    )


def grid_order(tokens):
    row = lax.broadcasted_iota(jnp.int32, (tokens, tokens), 0)
    col = lax.broadcasted_iota(jnp.int32, (tokens, tokens), 1)
    return row, col


def segments():
    head = lax.broadcasted_iota(jnp.int32, (HEADS, GROUP), 0)
    lane = lax.broadcasted_iota(jnp.int32, (HEADS, GROUP), 1)
    return jnp.where(lane // P_SIZE == head, 1.0, 0.0).astype(BF16)


def entry_of(cum_t):
    keep = cum_t[:, HEADS : HEADS + 1] < 0.5
    entry = jnp.where(keep, jnp.exp(cum_t[:, :HEADS]), 0.0)
    return mm(entry.astype(BF16), segments())


def tail_of(cum_t):
    last = cum_t[-1:, :]
    keep = cum_t[:, HEADS : HEADS + 1] == last[:, HEADS : HEADS + 1]
    tail = jnp.where(keep, jnp.exp(last[:, :HEADS] - cum_t[:, :HEADS]), 0.0)
    return mm(tail.astype(BF16), segments())


def local_state_kernel(decay_ref, x_ref, b_ref, state_ref, cum_ref, cum_t_ref):
    tokens = x_ref.shape[0]
    row, col = grid_order(tokens)
    decay = decay_ref[...]
    cum_ref[...] = exact(decay, jnp.where(row <= col, 1.0, 0.0))
    cum_t = exact(jnp.where(col <= row, 1.0, 0.0), decay, NT)
    cum_t_ref[...] = cum_t
    weighted = (x_ref[...].astype(F32) * tail_of(cum_t)).astype(BF16)
    state_ref[...] = mm(b_ref[...], weighted, TN).astype(BF16)


def forward_kernel(
    x_ref, b_ref, c_ref, z_ref, cum_ref, cum_t_ref, state_ref, gain_ref, y_ref, normed_ref
):
    tokens = x_ref.shape[0]
    row, col = grid_order(tokens)
    cum = cum_ref[...]
    cum_t = cum_t_ref[...]
    same = (col <= row) & (cum_t[:, HEADS : HEADS + 1] == cum[HEADS : HEADS + 1, :])
    scores = mm(c_ref[...], b_ref[...], NT)
    y_ref[...] = mm(c_ref[...], state_ref[...]) * entry_of(cum_t)
    low = lax.broadcasted_iota(jnp.int32, (tokens, 2 * P_SIZE), 1) < P_SIZE
    zero = jnp.zeros((tokens, 2 * P_SIZE), BF16)

    def weights(head):
        spread = cum_t[:, head : head + 1] - cum[head : head + 1, :]
        return (jnp.exp(jnp.where(same, spread, -1e30)) * scores).astype(BF16)

    for pair in range(HEADS // 2):
        lanes = slice(pair * 2 * P_SIZE, (pair + 1) * 2 * P_SIZE)
        x_pair = x_ref[:, lanes]
        y_ref[:, lanes] += mm(weights(2 * pair), jnp.where(low, x_pair, zero)) + mm(
            weights(2 * pair + 1), jnp.where(low, zero, x_pair)
        )
    z = z_ref[...].astype(F32)
    gated = y_ref[...] * (z / (1.0 + jnp.exp(-z)))
    scale = lax.rsqrt(jnp.mean(gated * gated, axis=1, keepdims=True) + 1e-05)
    normed_ref[...] = (gated * scale * gain_ref[...]).astype(BF16)


def norm_grad_kernel(
    y_ref, z_ref, gain_ref, grad_ref, c_ref, cum_t_ref, dy_ref, dz_ref, adjoint_ref
):
    z = z_ref[...].astype(F32)
    y = y_ref[...]
    sig = 1.0 / (1.0 + jnp.exp(-z))
    silu = z * sig
    gated = y * silu
    scale = lax.rsqrt(jnp.mean(gated * gated, axis=1, keepdims=True) + 1e-05)
    up = grad_ref[...].astype(F32) * gain_ref[...]
    shared = jnp.mean(up * gated, axis=1, keepdims=True)
    d_gated = scale * (up - gated * (scale * scale * shared))
    dz_ref[...] = d_gated * y * (sig * (1.0 + z * (1.0 - sig)))
    dy = d_gated * silu
    dy_ref[...] = dy.astype(BF16)
    adjoint_ref[...] = mm(
        c_ref[...], (dy * entry_of(cum_t_ref[...])).astype(BF16), TN
    ).astype(BF16)


def scan_grad_kernel(
    x_ref, b_ref, c_ref, dy_ref, cum_ref, cum_t_ref, state_ref, adjoint_ref,
    dx_ref, db_ref, dc_ref, decay_ref,
):
    tokens = x_ref.shape[0]
    row, col = grid_order(tokens)
    cum = cum_ref[...]
    cum_t = cum_t_ref[...]
    b = b_ref[...]
    c = c_ref[...]
    segment = segments()
    state = state_ref[...]
    adjoint = adjoint_ref[...]
    same = (row <= col) & (cum_t[:, HEADS : HEADS + 1] == cum[HEADS : HEADS + 1, :])
    scores = mm(b, c, NT)
    after = jnp.where(row >= col, 1.0, 0.0)
    after_bf = after.astype(BF16)
    before = row < col
    low = lax.broadcasted_iota(jnp.int32, (tokens, 2 * P_SIZE), 1) < P_SIZE
    zero = jnp.zeros((tokens, 2 * P_SIZE), BF16)

    tail = tail_of(cum_t)
    tail_x = x_ref[...].astype(F32) * tail
    back = mm(b, adjoint)
    dx_ref[...] = back * tail
    tail_sum = mm(segment, (tail_x * back).astype(BF16), NT)
    db_tail = mm(tail_x.astype(BF16), adjoint, NT)
    entry_dy = dy_ref[...].astype(F32) * entry_of(cum_t)
    entry_sum = mm(segment, (entry_dy * mm(c, state)).astype(BF16), NT)
    dc_entry = mm(entry_dy.astype(BF16), state, NT)
    through = mm(segment, (adjoint.astype(F32) * state.astype(F32)).astype(BF16), NT)
    through = jnp.sum(through, axis=1, keepdims=True)
    whole = jnp.where(
        cum[HEADS : HEADS + 1, -1:] < 0.5, jnp.exp(cum[:HEADS, -1:]), 0.0
    )
    decay_ref[...] = (
        exact(entry_sum, after) + exact(tail_sum, 1.0 - after) + whole * through
    )

    d_scores = jnp.zeros((tokens, tokens), F32)
    for pair in range(HEADS // 2):
        lanes = slice(pair * 2 * P_SIZE, (pair + 1) * 2 * P_SIZE)
        x_pair = x_ref[:, lanes]
        dy_pair = dy_ref[:, lanes]
        add = jnp.zeros((tokens, 2 * P_SIZE), F32)
        for half in range(2):
            head = 2 * pair + half
            dy_half = jnp.where(low, dy_pair, zero) if half == 0 else jnp.where(low, zero, dy_pair)
            spread = cum[head : head + 1, :] - cum_t[:, head : head + 1]
            weight = jnp.exp(jnp.where(same, spread, -1e30))
            weighted = weight * scores
            add += mm(weighted.astype(BF16), dy_half)
            d_weighted = mm(x_pair, dy_half, NT)
            d_scores += d_weighted * weight
            spans = mm((d_weighted * weighted).astype(BF16), after_bf)
            decay_ref[head : head + 1, :] += jnp.sum(
                jnp.where(before, spans, 0.0), axis=0, keepdims=True
            )
        dx_ref[:, lanes] += add
    d_scores = d_scores.astype(BF16)
    db_ref[...] = mm(d_scores, c) + db_tail
    dc_ref[...] = mm(d_scores, b, TN) + dc_entry


def group_specs(shapes):
    def spec(kind, tokens):
        if kind == "wide":
            return pl.BlockSpec((tokens, GROUP), lambda g: (0, g))
        if kind == "narrow":
            return pl.BlockSpec((tokens, N), lambda g: (0, g))
        if kind == "state":
            return pl.BlockSpec((N, GROUP), lambda g: (0, g))
        if kind == "gain":
            return pl.BlockSpec((1, GROUP), lambda g: (0, g))
        if kind == "rows":
            return pl.BlockSpec((None, ROWS, tokens), lambda g: (g, 0, 0))
        if kind == "columns":
            return pl.BlockSpec((None, tokens, ROWS), lambda g: (g, 0, 0))
        return pl.BlockSpec((HEADS, tokens), lambda g: (g, 0))

    return [spec(kind, tokens) for kind, tokens in shapes]


def run(kernel, groups, tokens, in_kinds, out_kinds, dtypes, flops, *args):
    shape = {
        "wide": (tokens, groups * GROUP),
        "narrow": (tokens, groups * N),
        "state": (N, groups * GROUP),
        "rows": (groups, ROWS, tokens),
        "columns": (groups, tokens, ROWS),
        "heads": (groups * HEADS, tokens),
    }
    return pl.pallas_call(
        kernel,
        grid=(groups,),
        in_specs=group_specs([(k, tokens) for k in in_kinds]),
        out_specs=group_specs([(k, tokens) for k in out_kinds]),
        out_shape=[jax.ShapeDtypeStruct(shape[k], d) for k, d in zip(out_kinds, dtypes)],
        cost_estimate=pl.CostEstimate(
            flops=flops * groups, bytes_accessed=4 * tokens * GROUP * groups * 4,
            transcendentals=tokens * tokens * HEADS * groups,
        ),
        compiler_params=pltpu.CompilerParams(vmem_limit_bytes=48 << 20),
    )(*args)


def pass_states(local, decays, reverse):
    count = lax.axis_size("seq")
    slices = lax.all_to_all(local, "seq", 0, 0, tiled=True)
    slices = slices.reshape(count, N // count, -1).astype(F32)
    factor = jnp.repeat(decays, P_SIZE, axis=1)
    carried = jnp.zeros(slices.shape[1:], F32)
    incoming = [None] * count
    for step in range(count):
        here = count - 1 - step if reverse else step
        incoming[here] = carried.astype(BF16)
        carried = factor[here][None, :] * carried + slices[here]
    return lax.all_to_all(jnp.concatenate(incoming, axis=0), "seq", 0, 0, tiled=True)


def per_device(
    inputs_x, inputs_b, inputs_c, gate_z, log_decay, resets, norm_gain, out_weight, out_grad
):
    tokens, width = inputs_x.shape
    groups = width // GROUP
    square = 2 * tokens * tokens * GROUP
    gain = norm_gain[None, :]

    full_weight = lax.all_gather(out_weight, "seq", axis=0, tiled=True)
    grad_full = lax.all_gather(out_grad, "head", axis=1, tiled=True)
    whole = jnp.exp(jnp.sum(log_decay, axis=1)) * (jnp.sum(resets) == 0).astype(F32)
    decays = lax.all_gather(whole, "seq", axis=0)

    decay_rows = jnp.concatenate(
        [
            log_decay.reshape(groups, HEADS, tokens),
            jnp.broadcast_to(resets.astype(F32)[None, None, :], (groups, 8, tokens)),
        ],
        axis=1,
    )
    local, cum, cum_t = run(
        local_state_kernel, groups, tokens, ("rows", "wide", "narrow"),
        ("state", "rows", "columns"), (BF16, F32, F32), square,
        decay_rows, inputs_x, inputs_b,
    )
    state_in = pass_states(local, decays, False)
    y, normed_bf = run(
        forward_kernel, groups, tokens,
        ("wide", "narrow", "narrow", "wide", "rows", "columns", "state", "gain"),
        ("wide", "wide"), (F32, BF16), 3 * square,
        inputs_x, inputs_b, inputs_c, gate_z, cum, cum_t, state_in, gain,
    )
    grad_weight = lax.psum_scatter(
        mm(grad_full, normed_bf, TN).astype(BF16), "seq", scatter_dimension=0, tiled=True
    ).astype(F32)
    grad_y = mm(grad_full, full_weight)
    dy, grad_z, adjoint = run(
        norm_grad_kernel, groups, tokens,
        ("wide", "wide", "gain", "wide", "narrow", "columns"),
        ("wide", "wide", "state"), (BF16, F32, BF16), square,
        y, gate_z, gain, grad_y, inputs_c, cum_t,
    )
    layer_out = lax.psum_scatter(
        mm(normed_bf, full_weight, NT).astype(BF16), "head", scatter_dimension=1, tiled=True
    )
    adjoint_out = pass_states(adjoint, decays, True)
    grad_x, grad_b, grad_c, grad_decay = run(
        scan_grad_kernel, groups, tokens,
        ("wide", "narrow", "narrow", "wide", "rows", "columns", "state", "state"),
        ("wide", "narrow", "narrow", "heads"), (F32, F32, F32, F32), 10 * square,
        inputs_x, inputs_b, inputs_c, dy, cum, cum_t, state_in, adjoint_out,
    )
    return (layer_out, grad_x, grad_b, grad_c, grad_z, grad_decay, grad_weight)


def solution(mesh):
    wide = P("seq", "head")
    return jax.shard_map(
        per_device,
        mesh=mesh,
        in_specs=(wide, wide, wide, wide, P("head", "seq"), P("seq"), P("head"), wide, wide),
        out_specs=(wide, wide, wide, wide, wide, P("head", "seq"), wide),
        check_vma=False,
    )
```

```python
import jax
import jax.numpy as jnp
from jax import lax
from jax.experimental import pallas as pl
from jax.experimental.pallas import tpu as pltpu
from jax.sharding import PartitionSpec as P

P_SIZE = 64
N = 128
GROUP = 1024
HEADS = GROUP // P_SIZE
ROWS = HEADS + 8
F32 = jnp.float32
BF16 = jnp.bfloat16
NN = (((1,), (0,)), ((), ()))
NT = (((1,), (1,)), ((), ()))
TN = (((0,), (0,)), ((), ()))


def mm(a, b, dims=NN):
    return lax.dot_general(a, b, dims, preferred_element_type=F32)


def exact(a, b, dims=NN):
    return lax.dot_general(
        a, b, dims, preferred_element_type=F32, precision=lax.Precision.HIGHEST
    )


def grid_order(tokens):
    row = lax.broadcasted_iota(jnp.int32, (tokens, tokens), 0)
    col = lax.broadcasted_iota(jnp.int32, (tokens, tokens), 1)
    return row, col


def segments():
    head = lax.broadcasted_iota(jnp.int32, (HEADS, GROUP), 0)
    lane = lax.broadcasted_iota(jnp.int32, (HEADS, GROUP), 1)
    return jnp.where(lane // P_SIZE == head, 1.0, 0.0).astype(BF16)


def entry_of(cum_t):
    keep = cum_t[:, HEADS : HEADS + 1] < 0.5
    entry = jnp.where(keep, jnp.exp(cum_t[:, :HEADS]), 0.0)
    return mm(entry.astype(BF16), segments())


def tail_of(cum_t):
    last = cum_t[-1:, :]
    keep = cum_t[:, HEADS : HEADS + 1] == last[:, HEADS : HEADS + 1]
    tail = jnp.where(keep, jnp.exp(last[:, :HEADS] - cum_t[:, :HEADS]), 0.0)
    return mm(tail.astype(BF16), segments())


def local_state_kernel(decay_ref, x_ref, b_ref, state_ref, cum_ref, cum_t_ref):
    tokens = x_ref.shape[0]
    row, col = grid_order(tokens)
    decay = decay_ref[...]
    cum_ref[...] = exact(decay, jnp.where(row <= col, 1.0, 0.0))
    cum_t = exact(jnp.where(col <= row, 1.0, 0.0), decay, NT)
    cum_t_ref[...] = cum_t
    weighted = (x_ref[...].astype(F32) * tail_of(cum_t)).astype(BF16)
    state_ref[...] = mm(b_ref[...], weighted, TN).astype(BF16)


def forward_kernel(
    x_ref, b_ref, c_ref, z_ref, cum_ref, cum_t_ref, state_ref, gain_ref, y_ref, normed_ref
):
    tokens = x_ref.shape[0]
    row, col = grid_order(tokens)
    cum = cum_ref[...]
    cum_t = cum_t_ref[...]
    same = (col <= row) & (cum_t[:, HEADS : HEADS + 1] == cum[HEADS : HEADS + 1, :])
    scores = mm(c_ref[...], b_ref[...], NT)
    y_ref[...] = mm(c_ref[...], state_ref[...]) * entry_of(cum_t)
    low = lax.broadcasted_iota(jnp.int32, (tokens, 2 * P_SIZE), 1) < P_SIZE
    zero = jnp.zeros((tokens, 2 * P_SIZE), BF16)

    def weights(head):
        spread = cum_t[:, head : head + 1] - cum[head : head + 1, :]
        return (jnp.exp(jnp.where(same, spread, -1e30)) * scores).astype(BF16)

    for pair in range(HEADS // 2):
        lanes = slice(pair * 2 * P_SIZE, (pair + 1) * 2 * P_SIZE)
        x_pair = x_ref[:, lanes]
        y_ref[:, lanes] += mm(weights(2 * pair), jnp.where(low, x_pair, zero)) + mm(
            weights(2 * pair + 1), jnp.where(low, zero, x_pair)
        )
    z = z_ref[...].astype(F32)
    gated = y_ref[...] * (z / (1.0 + jnp.exp(-z)))
    scale = lax.rsqrt(jnp.mean(gated * gated, axis=1, keepdims=True) + 1e-05)
    normed_ref[...] = (gated * scale * gain_ref[...]).astype(BF16)


def norm_grad_kernel(
    y_ref, z_ref, gain_ref, grad_ref, c_ref, cum_t_ref, dy_ref, dz_ref, adjoint_ref
):
    z = z_ref[...].astype(F32)
    y = y_ref[...]
    sig = 1.0 / (1.0 + jnp.exp(-z))
    silu = z * sig
    gated = y * silu
    scale = lax.rsqrt(jnp.mean(gated * gated, axis=1, keepdims=True) + 1e-05)
    up = grad_ref[...].astype(F32) * gain_ref[...]
    shared = jnp.mean(up * gated, axis=1, keepdims=True)
    d_gated = scale * (up - gated * (scale * scale * shared))
    dz_ref[...] = d_gated * y * (sig * (1.0 + z * (1.0 - sig)))
    dy = d_gated * silu
    dy_ref[...] = dy.astype(BF16)
    adjoint_ref[...] = mm(
        c_ref[...], (dy * entry_of(cum_t_ref[...])).astype(BF16), TN
    ).astype(BF16)


def scan_grad_kernel(
    x_ref, b_ref, c_ref, dy_ref, cum_ref, cum_t_ref, state_ref, adjoint_ref,
    dx_ref, db_ref, dc_ref, decay_ref,
):
    tokens = x_ref.shape[0]
    row, col = grid_order(tokens)
    cum = cum_ref[...]
    cum_t = cum_t_ref[...]
    b = b_ref[...]
    c = c_ref[...]
    segment = segments()
    state = state_ref[...]
    adjoint = adjoint_ref[...]
    same = (row <= col) & (cum_t[:, HEADS : HEADS + 1] == cum[HEADS : HEADS + 1, :])
    scores = mm(b, c, NT)
    after = jnp.where(row >= col, 1.0, 0.0)
    after_bf = after.astype(BF16)
    before = row < col
    low = lax.broadcasted_iota(jnp.int32, (tokens, 2 * P_SIZE), 1) < P_SIZE
    zero = jnp.zeros((tokens, 2 * P_SIZE), BF16)

    tail = tail_of(cum_t)
    tail_x = x_ref[...].astype(F32) * tail
    back = mm(b, adjoint)
    dx_ref[...] = back * tail
    tail_sum = mm(segment, (tail_x * back).astype(BF16), NT)
    db_tail = mm(tail_x.astype(BF16), adjoint, NT)
    entry_dy = dy_ref[...].astype(F32) * entry_of(cum_t)
    entry_sum = mm(segment, (entry_dy * mm(c, state)).astype(BF16), NT)
    dc_entry = mm(entry_dy.astype(BF16), state, NT)
    through = mm(segment, (adjoint.astype(F32) * state.astype(F32)).astype(BF16), NT)
    through = jnp.sum(through, axis=1, keepdims=True)
    whole = jnp.where(
        cum[HEADS : HEADS + 1, -1:] < 0.5, jnp.exp(cum[:HEADS, -1:]), 0.0
    )
    decay_ref[...] = (
        exact(entry_sum, after) + exact(tail_sum, 1.0 - after) + whole * through
    )

    d_scores = jnp.zeros((tokens, tokens), F32)
    for pair in range(HEADS // 2):
        lanes = slice(pair * 2 * P_SIZE, (pair + 1) * 2 * P_SIZE)
        x_pair = x_ref[:, lanes]
        dy_pair = dy_ref[:, lanes]
        add = jnp.zeros((tokens, 2 * P_SIZE), F32)
        for half in range(2):
            head = 2 * pair + half
            dy_half = jnp.where(low, dy_pair, zero) if half == 0 else jnp.where(low, zero, dy_pair)
            spread = cum[head : head + 1, :] - cum_t[:, head : head + 1]
            weight = jnp.exp(jnp.where(same, spread, -1e30))
            weighted = weight * scores
            add += mm(weighted.astype(BF16), dy_half)
            d_weighted = mm(x_pair, dy_half, NT)
            d_scores += d_weighted * weight
            spans = mm((d_weighted * weighted).astype(BF16), after_bf)
            decay_ref[head : head + 1, :] += jnp.sum(
                jnp.where(before, spans, 0.0), axis=0, keepdims=True
            )
        dx_ref[:, lanes] += add
    d_scores = d_scores.astype(BF16)
    db_ref[...] = mm(d_scores, c) + db_tail
    dc_ref[...] = mm(d_scores, b, TN) + dc_entry


def group_specs(shapes):
    def spec(kind, tokens):
        if kind == "wide":
            return pl.BlockSpec((tokens, GROUP), lambda g: (0, g))
        if kind == "narrow":
            return pl.BlockSpec((tokens, N), lambda g: (0, g))
        if kind == "state":
            return pl.BlockSpec((N, GROUP), lambda g: (0, g))
        if kind == "gain":
            return pl.BlockSpec((1, GROUP), lambda g: (0, g))
        if kind == "rows":
            return pl.BlockSpec((None, ROWS, tokens), lambda g: (g, 0, 0))
        if kind == "columns":
            return pl.BlockSpec((None, tokens, ROWS), lambda g: (g, 0, 0))
        return pl.BlockSpec((HEADS, tokens), lambda g: (g, 0))

    return [spec(kind, tokens) for kind, tokens in shapes]


def run(kernel, groups, tokens, in_kinds, out_kinds, dtypes, flops, *args):
    shape = {
        "wide": (tokens, groups * GROUP),
        "narrow": (tokens, groups * N),
        "state": (N, groups * GROUP),
        "rows": (groups, ROWS, tokens),
        "columns": (groups, tokens, ROWS),
        "heads": (groups * HEADS, tokens),
    }
    return pl.pallas_call(
        kernel,
        grid=(groups,),
        in_specs=group_specs([(k, tokens) for k in in_kinds]),
        out_specs=group_specs([(k, tokens) for k in out_kinds]),
        out_shape=[jax.ShapeDtypeStruct(shape[k], d) for k, d in zip(out_kinds, dtypes)],
        cost_estimate=pl.CostEstimate(
            flops=flops * groups, bytes_accessed=4 * tokens * GROUP * groups * 4,
            transcendentals=tokens * tokens * HEADS * groups,
        ),
        compiler_params=pltpu.CompilerParams(vmem_limit_bytes=48 << 20),
    )(*args)


def pass_states(local, decays, reverse):
    count = lax.axis_size("seq")
    slices = lax.all_to_all(local, "seq", 0, 0, tiled=True)
    slices = slices.reshape(count, N // count, -1).astype(F32)
    factor = jnp.repeat(decays, P_SIZE, axis=1)
    carried = jnp.zeros(slices.shape[1:], F32)
    incoming = [None] * count
    for step in range(count):
        here = count - 1 - step if reverse else step
        incoming[here] = carried.astype(BF16)
        carried = factor[here][None, :] * carried + slices[here]
    return lax.all_to_all(jnp.concatenate(incoming, axis=0), "seq", 0, 0, tiled=True)


def shift(value, steps):
    count = lax.axis_size("head")
    return lax.ppermute(value, "head", [(i, (i + steps) % count) for i in range(count)])


def gather_heads(value):
    count = lax.axis_size("head")
    width = value.shape[1]
    me = lax.axis_index("head")
    whole = jnp.zeros((value.shape[0], count * width), value.dtype)
    for steps in range(count):
        block = shift(value, steps) if steps else value
        whole = lax.dynamic_update_slice(whole, block, (0, (me - steps) % count * width))
    return whole


def project(normed, weight):
    count = lax.axis_size("head")
    rows = weight.shape[0] // count
    me = lax.axis_index("head")
    total = None
    for steps in list(range(1, count)) + [0]:
        block = lax.dynamic_slice(
            weight, ((me + steps) % count * rows, 0), (rows, weight.shape[1])
        )
        term = mm(normed, block, NT).astype(BF16)
        term = (shift(term, steps) if steps else term).astype(F32)
        total = term if total is None else total + term
    return total.astype(BF16)


def per_device(
    inputs_x, inputs_b, inputs_c, gate_z, log_decay, resets, norm_gain, out_weight, out_grad
):
    tokens, width = inputs_x.shape
    groups = width // GROUP
    square = 2 * tokens * tokens * GROUP
    gain = norm_gain[None, :]

    full_weight = lax.all_gather(out_weight, "seq", axis=0, tiled=True)
    grad_full = gather_heads(out_grad)
    grad_columns = lax.all_to_all(grad_full, "seq", 1, 0, tiled=True)
    whole = jnp.exp(jnp.sum(log_decay, axis=1)) * (jnp.sum(resets) == 0).astype(F32)
    count = lax.axis_size("seq")
    decays = lax.all_to_all(
        jnp.broadcast_to(whole[None, :], (count, whole.shape[0])), "seq", 0, 0, tiled=True
    )

    decay_rows = jnp.concatenate(
        [
            log_decay.reshape(groups, HEADS, tokens),
            jnp.broadcast_to(resets.astype(F32)[None, None, :], (groups, 8, tokens)),
        ],
        axis=1,
    )
    local, cum, cum_t = run(
        local_state_kernel, groups, tokens, ("rows", "wide", "narrow"),
        ("state", "rows", "columns"), (BF16, F32, F32), square,
        decay_rows, inputs_x, inputs_b,
    )
    state_in = pass_states(local, decays, False)
    y, normed_bf = run(
        forward_kernel, groups, tokens,
        ("wide", "narrow", "narrow", "wide", "rows", "columns", "state", "gain"),
        ("wide", "wide"), (F32, BF16), 3 * square,
        inputs_x, inputs_b, inputs_c, gate_z, cum, cum_t, state_in, gain,
    )
    sent, full_weight, grad_columns = lax.optimization_barrier(
        (normed_bf, full_weight, grad_columns)
    )
    normed_all = lax.all_gather(sent, "seq", axis=0, tiled=True)
    grad_y = mm(grad_full, full_weight)
    dy, grad_z, adjoint = run(
        norm_grad_kernel, groups, tokens,
        ("wide", "wide", "gain", "wide", "narrow", "columns"),
        ("wide", "wide", "state"), (BF16, F32, BF16), square,
        y, gate_z, gain, grad_y, inputs_c, cum_t,
    )
    layer_out = project(normed_bf, full_weight)
    adjoint_out = pass_states(adjoint, decays, True)
    grad_x, grad_b, grad_c, grad_decay = run(
        scan_grad_kernel, groups, tokens,
        ("wide", "narrow", "narrow", "wide", "rows", "columns", "state", "state"),
        ("wide", "narrow", "narrow", "heads"), (F32, F32, F32, F32), 10 * square,
        inputs_x, inputs_b, inputs_c, dy, cum, cum_t, state_in, adjoint_out,
    )
    grad_weight = mm(grad_columns, normed_all, TN)
    return (layer_out, grad_x, grad_b, grad_c, grad_z, grad_decay, grad_weight)


def solution(mesh):
    wide = P("seq", "head")
    return jax.shard_map(
        per_device,
        mesh=mesh,
        in_specs=(wide, wide, wide, wide, P("head", "seq"), P("seq"), P("head"), wide, wide),
        out_specs=(wide, wide, wide, wide, wide, P("head", "seq"), wide),
        check_vma=False,
    )
```

```python
import jax
import jax.numpy as jnp
from jax import lax
from jax.experimental import pallas as pl
from jax.experimental.pallas import tpu as pltpu
from jax.sharding import PartitionSpec as P

P_SIZE = 64
N = 128
GROUP = 1024
HEADS = GROUP // P_SIZE
ROWS = HEADS + 8
F32 = jnp.float32
BF16 = jnp.bfloat16
NN = (((1,), (0,)), ((), ()))
NT = (((1,), (1,)), ((), ()))
TN = (((0,), (0,)), ((), ()))


def mm(a, b, dims=NN):
    return lax.dot_general(a, b, dims, preferred_element_type=F32)


def exact(a, b, dims=NN):
    return lax.dot_general(
        a, b, dims, preferred_element_type=F32, precision=lax.Precision.HIGHEST
    )


def grid_order(tokens):
    row = lax.broadcasted_iota(jnp.int32, (tokens, tokens), 0)
    col = lax.broadcasted_iota(jnp.int32, (tokens, tokens), 1)
    return row, col


def segments():
    head = lax.broadcasted_iota(jnp.int32, (HEADS, GROUP), 0)
    lane = lax.broadcasted_iota(jnp.int32, (HEADS, GROUP), 1)
    return jnp.where(lane // P_SIZE == head, 1.0, 0.0).astype(BF16)


def entry_of(cum_t):
    keep = cum_t[:, HEADS : HEADS + 1] < 0.5
    entry = jnp.where(keep, jnp.exp(cum_t[:, :HEADS]), 0.0)
    return mm(entry.astype(BF16), segments())


def tail_of(cum_t):
    last = cum_t[-1:, :]
    keep = cum_t[:, HEADS : HEADS + 1] == last[:, HEADS : HEADS + 1]
    tail = jnp.where(keep, jnp.exp(last[:, :HEADS] - cum_t[:, :HEADS]), 0.0)
    return mm(tail.astype(BF16), segments())


def local_state_kernel(decay_ref, x_ref, b_ref, state_ref, cum_ref, cum_t_ref):
    tokens = x_ref.shape[0]
    row, col = grid_order(tokens)
    decay = decay_ref[...]
    cum_ref[...] = exact(decay, jnp.where(row <= col, 1.0, 0.0))
    cum_t = exact(jnp.where(col <= row, 1.0, 0.0), decay, NT)
    cum_t_ref[...] = cum_t
    weighted = (x_ref[...].astype(F32) * tail_of(cum_t)).astype(BF16)
    state_ref[...] = mm(b_ref[...], weighted, TN).astype(BF16)


def forward_kernel(
    x_ref, b_ref, c_ref, z_ref, cum_ref, cum_t_ref, state_ref, gain_ref, y_ref, normed_ref
):
    tokens = x_ref.shape[0]
    row, col = grid_order(tokens)
    cum = cum_ref[...]
    cum_t = cum_t_ref[...]
    same = (col <= row) & (cum_t[:, HEADS : HEADS + 1] == cum[HEADS : HEADS + 1, :])
    scores = mm(c_ref[...], b_ref[...], NT)
    y_ref[...] = mm(c_ref[...], state_ref[...]) * entry_of(cum_t)
    low = lax.broadcasted_iota(jnp.int32, (tokens, 2 * P_SIZE), 1) < P_SIZE
    zero = jnp.zeros((tokens, 2 * P_SIZE), BF16)

    def weights(head):
        spread = cum_t[:, head : head + 1] - cum[head : head + 1, :]
        return (jnp.exp(jnp.where(same, spread, -1e30)) * scores).astype(BF16)

    for pair in range(HEADS // 2):
        lanes = slice(pair * 2 * P_SIZE, (pair + 1) * 2 * P_SIZE)
        x_pair = x_ref[:, lanes]
        y_ref[:, lanes] += mm(weights(2 * pair), jnp.where(low, x_pair, zero)) + mm(
            weights(2 * pair + 1), jnp.where(low, zero, x_pair)
        )
    z = z_ref[...].astype(F32)
    gated = y_ref[...] * (z / (1.0 + jnp.exp(-z)))
    scale = lax.rsqrt(jnp.mean(gated * gated, axis=1, keepdims=True) + 1e-05)
    normed_ref[...] = (gated * scale * gain_ref[...]).astype(BF16)


def norm_grad_kernel(
    y_ref, z_ref, gain_ref, grad_ref, c_ref, cum_t_ref, dy_ref, dz_ref, adjoint_ref
):
    z = z_ref[...].astype(F32)
    y = y_ref[...]
    sig = 1.0 / (1.0 + jnp.exp(-z))
    silu = z * sig
    gated = y * silu
    scale = lax.rsqrt(jnp.mean(gated * gated, axis=1, keepdims=True) + 1e-05)
    up = grad_ref[...].astype(F32) * gain_ref[...]
    shared = jnp.mean(up * gated, axis=1, keepdims=True)
    d_gated = scale * (up - gated * (scale * scale * shared))
    dz_ref[...] = d_gated * y * (sig * (1.0 + z * (1.0 - sig)))
    dy = d_gated * silu
    dy_ref[...] = dy.astype(BF16)
    adjoint_ref[...] = mm(
        c_ref[...], (dy * entry_of(cum_t_ref[...])).astype(BF16), TN
    ).astype(BF16)


def scan_grad_kernel(
    x_ref, b_ref, c_ref, dy_ref, cum_ref, cum_t_ref, state_ref, adjoint_ref,
    dx_ref, db_ref, dc_ref, decay_ref,
):
    tokens = x_ref.shape[0]
    row, col = grid_order(tokens)
    cum = cum_ref[...]
    cum_t = cum_t_ref[...]
    b = b_ref[...]
    c = c_ref[...]
    segment = segments()
    state = state_ref[...]
    adjoint = adjoint_ref[...]
    same = (row <= col) & (cum_t[:, HEADS : HEADS + 1] == cum[HEADS : HEADS + 1, :])
    scores = mm(b, c, NT)
    after = jnp.where(row >= col, 1.0, 0.0)
    after_bf = after.astype(BF16)
    before = row < col
    low = lax.broadcasted_iota(jnp.int32, (tokens, 2 * P_SIZE), 1) < P_SIZE
    zero = jnp.zeros((tokens, 2 * P_SIZE), BF16)

    tail = tail_of(cum_t)
    tail_x = x_ref[...].astype(F32) * tail
    back = mm(b, adjoint)
    dx_ref[...] = back * tail
    tail_sum = mm(segment, (tail_x * back).astype(BF16), NT)
    db_tail = mm(tail_x.astype(BF16), adjoint, NT)
    entry_dy = dy_ref[...].astype(F32) * entry_of(cum_t)
    entry_sum = mm(segment, (entry_dy * mm(c, state)).astype(BF16), NT)
    dc_entry = mm(entry_dy.astype(BF16), state, NT)
    through = mm(segment, (adjoint.astype(F32) * state.astype(F32)).astype(BF16), NT)
    through = jnp.sum(through, axis=1, keepdims=True)
    whole = jnp.where(
        cum[HEADS : HEADS + 1, -1:] < 0.5, jnp.exp(cum[:HEADS, -1:]), 0.0
    )
    decay_ref[...] = (
        exact(entry_sum, after) + exact(tail_sum, 1.0 - after) + whole * through
    )

    d_scores = jnp.zeros((tokens, tokens), F32)
    for pair in range(HEADS // 2):
        lanes = slice(pair * 2 * P_SIZE, (pair + 1) * 2 * P_SIZE)
        x_pair = x_ref[:, lanes]
        dy_pair = dy_ref[:, lanes]
        add = jnp.zeros((tokens, 2 * P_SIZE), F32)
        for half in range(2):
            head = 2 * pair + half
            dy_half = jnp.where(low, dy_pair, zero) if half == 0 else jnp.where(low, zero, dy_pair)
            spread = cum[head : head + 1, :] - cum_t[:, head : head + 1]
            weight = jnp.exp(jnp.where(same, spread, -1e30))
            weighted = weight * scores
            add += mm(weighted.astype(BF16), dy_half)
            d_weighted = mm(x_pair, dy_half, NT)
            d_scores += d_weighted * weight
            spans = mm((d_weighted * weighted).astype(BF16), after_bf)
            decay_ref[head : head + 1, :] += jnp.sum(
                jnp.where(before, spans, 0.0), axis=0, keepdims=True
            )
        dx_ref[:, lanes] += add
    d_scores = d_scores.astype(BF16)
    db_ref[...] = mm(d_scores, c) + db_tail
    dc_ref[...] = mm(d_scores, b, TN) + dc_entry


def group_specs(shapes):
    def spec(kind, tokens):
        if kind == "wide":
            return pl.BlockSpec((tokens, GROUP), lambda g: (0, g))
        if kind == "narrow":
            return pl.BlockSpec((tokens, N), lambda g: (0, g))
        if kind == "state":
            return pl.BlockSpec((N, GROUP), lambda g: (0, g))
        if kind == "gain":
            return pl.BlockSpec((1, GROUP), lambda g: (0, g))
        if kind == "rows":
            return pl.BlockSpec((None, ROWS, tokens), lambda g: (g, 0, 0))
        if kind == "columns":
            return pl.BlockSpec((None, tokens, ROWS), lambda g: (g, 0, 0))
        return pl.BlockSpec((HEADS, tokens), lambda g: (g, 0))

    return [spec(kind, tokens) for kind, tokens in shapes]


def run(kernel, groups, tokens, in_kinds, out_kinds, dtypes, flops, *args):
    shape = {
        "wide": (tokens, groups * GROUP),
        "narrow": (tokens, groups * N),
        "state": (N, groups * GROUP),
        "rows": (groups, ROWS, tokens),
        "columns": (groups, tokens, ROWS),
        "heads": (groups * HEADS, tokens),
    }
    return pl.pallas_call(
        kernel,
        grid=(groups,),
        in_specs=group_specs([(k, tokens) for k in in_kinds]),
        out_specs=group_specs([(k, tokens) for k in out_kinds]),
        out_shape=[jax.ShapeDtypeStruct(shape[k], d) for k, d in zip(out_kinds, dtypes)],
        cost_estimate=pl.CostEstimate(
            flops=flops * groups, bytes_accessed=4 * tokens * GROUP * groups * 4,
            transcendentals=tokens * tokens * HEADS * groups,
        ),
        compiler_params=pltpu.CompilerParams(vmem_limit_bytes=48 << 20),
    )(*args)


def pass_states(local, decays, reverse):
    count = lax.axis_size("seq")
    slices = lax.all_to_all(local, "seq", 0, 0, tiled=True)
    slices = slices.reshape(count, N // count, -1).astype(F32)
    factor = jnp.repeat(decays, P_SIZE, axis=1)
    carried = jnp.zeros(slices.shape[1:], F32)
    incoming = [None] * count
    for step in range(count):
        here = count - 1 - step if reverse else step
        incoming[here] = carried.astype(BF16)
        carried = factor[here][None, :] * carried + slices[here]
    return lax.all_to_all(jnp.concatenate(incoming, axis=0), "seq", 0, 0, tiled=True)


def shift(value, steps):
    count = lax.axis_size("head")
    return lax.ppermute(value, "head", [(i, (i + steps) % count) for i in range(count)])


def gather_heads(value):
    count = lax.axis_size("head")
    width = value.shape[1]
    me = lax.axis_index("head")
    whole = jnp.zeros((value.shape[0], count * width), value.dtype)
    for steps in range(count):
        block = shift(value, steps) if steps else value
        whole = lax.dynamic_update_slice(whole, block, (0, (me - steps) % count * width))
    return whole


def project(normed, weight):
    count = lax.axis_size("head")
    rows = weight.shape[0] // count
    me = lax.axis_index("head")
    terms = []
    for steps in range(count):
        block = lax.dynamic_slice(
            weight, ((me + steps) % count * rows, 0), (rows, weight.shape[1])
        )
        term = mm(normed, block, NT).astype(BF16)
        terms.append(shift(term, steps) if steps else term)
    return terms


def per_device(
    inputs_x, inputs_b, inputs_c, gate_z, log_decay, resets, norm_gain, out_weight, out_grad
):
    tokens, width = inputs_x.shape
    groups = width // GROUP
    square = 2 * tokens * tokens * GROUP
    gain = norm_gain[None, :]

    full_weight = lax.all_gather(out_weight, "seq", axis=0, tiled=True)
    grad_full = gather_heads(out_grad)
    grad_columns = lax.all_to_all(grad_full, "seq", 1, 0, tiled=True)
    whole = jnp.exp(jnp.sum(log_decay, axis=1)) * (jnp.sum(resets) == 0).astype(F32)
    count = lax.axis_size("seq")
    decays = lax.all_to_all(
        jnp.broadcast_to(whole[None, :], (count, whole.shape[0])), "seq", 0, 0, tiled=True
    )

    decay_rows = jnp.concatenate(
        [
            log_decay.reshape(groups, HEADS, tokens),
            jnp.broadcast_to(resets.astype(F32)[None, None, :], (groups, 8, tokens)),
        ],
        axis=1,
    )
    local, cum, cum_t = run(
        local_state_kernel, groups, tokens, ("rows", "wide", "narrow"),
        ("state", "rows", "columns"), (BF16, F32, F32), square,
        decay_rows, inputs_x, inputs_b,
    )
    state_in = pass_states(local, decays, False)
    y, normed_bf = run(
        forward_kernel, groups, tokens,
        ("wide", "narrow", "narrow", "wide", "rows", "columns", "state", "gain"),
        ("wide", "wide"), (F32, BF16), 3 * square,
        inputs_x, inputs_b, inputs_c, gate_z, cum, cum_t, state_in, gain,
    )
    sent, full_weight, grad_columns = lax.optimization_barrier(
        (normed_bf, full_weight, grad_columns)
    )
    normed_all = lax.all_gather(sent, "seq", axis=0, tiled=True)
    grad_y = mm(grad_full, full_weight)
    dy, grad_z, adjoint = run(
        norm_grad_kernel, groups, tokens,
        ("wide", "wide", "gain", "wide", "narrow", "columns"),
        ("wide", "wide", "state"), (BF16, F32, BF16), square,
        y, gate_z, gain, grad_y, inputs_c, cum_t,
    )
    terms = project(normed_bf, full_weight)
    adjoint_out = pass_states(adjoint, decays, True)
    grad_x, grad_b, grad_c, grad_decay = run(
        scan_grad_kernel, groups, tokens,
        ("wide", "narrow", "narrow", "wide", "rows", "columns", "state", "state"),
        ("wide", "narrow", "narrow", "heads"), (F32, F32, F32, F32), 10 * square,
        inputs_x, inputs_b, inputs_c, dy, cum, cum_t, state_in, adjoint_out,
    )
    terms, grad_decay = lax.optimization_barrier((terms, grad_decay))
    layer_out = sum(term.astype(F32) for term in terms).astype(BF16)
    grad_weight = mm(grad_columns, normed_all, TN)
    return (layer_out, grad_x, grad_b, grad_c, grad_z, grad_decay, grad_weight)


def solution(mesh):
    wide = P("seq", "head")
    return jax.shard_map(
        per_device,
        mesh=mesh,
        in_specs=(wide, wide, wide, wide, P("head", "seq"), P("seq"), P("head"), wide, wide),
        out_specs=(wide, wide, wide, wide, wide, P("head", "seq"), wide),
        check_vma=False,
    )
```
